256 devices in a mesh: member: 16 (over x, z_hi), cell: 16 (over y, z_lo, core).
Axes of the slice: x: 4, y: 4, z: 8 (z_hi: 4, z_lo: 2; z = z_hi * 2 + z_lo), core: 2. Of those that a mesh axis runs over, the one named last changes fastest.
Arguments:
- latent: bfloat16 [16, 24576, 1024], P('member', 'cell'), may hold values from -6 to 6
- w_in: bfloat16 [1024, 1024], replicated, may hold values from -0.1875 to 0.1875
- w_out: bfloat16 [1024, 96], replicated, may hold values from -0.1875 to 0.1875
- target: bfloat16 [96, 24576], P(None, 'cell'), may hold values from -6 to 6
- cell_mask: int32 [24576], P('cell'), may hold values 0 or 1
Outputs:
- grad_w_in: float32 [1024, 1024], P(('member', 'cell'))
- grad_w_out: float32 [1024, 96], P(('member', 'cell'))
The draws below stay inside these ranges and needn't reach their ends.
All inputs are finite; a program needn't handle non-finite values. No bound on the sum of `cell_mask` on one device may be relied on, other than what follows from the above.
Results may differ from the reference program's by a relative error of at most 0.0055.
Values may be sent and summed in bfloat16 or wider, within the bound.
No kernel may reach another device: no remote copies, remote signals or barrier semaphores. Data moves between devices by JAX's collectives and lax.ppermute only.
A program may use at most 64 MiB of HBM per device.

```python
import jax
import jax.numpy as jnp
from jax import lax

LATENT = 1024
HIDDEN_SIZE = 1024
FIELDS = 96
CELLS = 24576
MEMBERS = 16


def plant(values, stream_key, low, top_value):
    longest = values.shape.index(max(values.shape))
    spots = []
    for shift in (0, 1):
        where = [jax.random.randint(jax.random.fold_in(stream_key, axis), (), 0, length) for axis, length in enumerate(values.shape)]
        where[longest] = (where[longest] + shift) % values.shape[longest]
        spots.append(tuple(where))
    return values.at[spots[0]].set(low).at[spots[1]].set(top_value)


def with_spikes(array, key, source, target, parts, factor):
    owner, partner = [(jnp.arange(array.shape[axis_at]) // (array.shape[axis_at] // parts)).reshape([-1 if axis == axis_at else 1 for axis in range(array.ndim)]) for axis_at in (source, target)]
    chosen = jax.random.permutation(key, parts)[partner]
    strong = (owner == chosen) | (owner == (partner + parts // 2) % parts)
    return jnp.where(strong, factor * array, array)


def levels(key, shape, shards, least, largest):
    def one(dim, shards_of):
        steps = jax.random.uniform(jax.random.fold_in(jax.random.fold_in(key, 6), dim), (shards_of,), jnp.float32, least / len(shards), largest / len(shards))
        return jnp.repeat(jnp.exp(steps), shape[dim] // shards_of).reshape((-1,) + (1,) * (len(shape) - dim - 1))

    factor_of = one(*shards[0])
    for cut in shards[1:]:
        factor_of = factor_of * one(*cut)
    return factor_of


def centred(key, extent, spread, reach, pieces=(), held_as=jnp.bfloat16):
    level = levels(key, extent, pieces, -0.22, 0.18) if pieces else 1.0
    result = jax.random.normal(key, extent, jnp.float32) * spread * level
    return jnp.minimum(jnp.maximum(result, -reach), reach).astype(held_as)


def heavy_noise(own_key, shape, deviation, most, cuts, heavy, dtype=jnp.bfloat16):
    values = deviation * jax.random.normal(own_key, shape, jnp.float32)
    if cuts:
        values = values * levels(own_key, shape, cuts, -0.22, 0.18)
    return jnp.clip(with_spikes(values, jax.random.fold_in(own_key, 3), *heavy), -most, most).astype(dtype)


def setup_inputs(seed: int = 0) -> dict:
    key_of = jax.random.split(jax.random.key(seed), 6)
    latent = heavy_noise(key_of[0], (MEMBERS, CELLS, LATENT), 1.0, 6.0, ((0, 16), (1, 16)), (1, 2, 16, 2.0))
    w_in = centred(key_of[1], (LATENT, HIDDEN_SIZE), LATENT ** -0.5, 0.1875)
    w_out = centred(key_of[2], (HIDDEN_SIZE, FIELDS), HIDDEN_SIZE ** -0.5, 0.1875)
    target = centred(key_of[3], (FIELDS, CELLS), 1.0, 6.0, ((1, 16),))
    cell_mask = plant((jax.random.randint(key_of[4], (CELLS,), 0, 4) < 3).astype(jnp.int32), jax.random.fold_in(key_of[4], 1), 0, 1)
    return dict(latent=latent, w_in=w_in, w_out=w_out, target=target, cell_mask=cell_mask)


def kernel_fn(diff):
    return diff / jnp.sqrt(1.0 + diff * diff)

def silu_slope(pre):
    gate = jax.nn.sigmoid(pre)
    return gate * (1.0 + pre * (1.0 - gate))

def decode(member_latent, w_in, w_out):
    pre = jnp.dot(member_latent, w_in, preferred_element_type=jnp.float32)
    hidden = jax.nn.silu(pre).astype(jnp.bfloat16)
    fields = lax.dot_general(w_out, hidden, (((0,), (1,)), ((), ())), preferred_element_type=jnp.float32).astype(jnp.bfloat16)
    return (pre, hidden, fields)

def reference(latent, w_in, w_out, target, cell_mask):
    members = latent.shape[0]
    cells = latent.shape[1]
    scale = 1.0 / jnp.sqrt(jnp.float32(cells))
    fields = lax.map(lambda one: decode(one, w_in, w_out)[2], latent)
    wide = fields.astype(jnp.float32)
    pair = lax.map(lambda own: lax.optimization_barrier(jnp.sum(kernel_fn(own[None] - wide), axis=0)), wide)
    weight = cell_mask.astype(jnp.float32) * scale / members
    own_term = kernel_fn(wide - target.astype(jnp.float32)[None])
    grad_fields = (weight[None, None] * (own_term - pair / members)).astype(jnp.bfloat16)

    def accumulate(carry, item):
        member_latent, member_grad = item
        pre, hidden, unused = decode(member_latent, w_in, w_out)
        back = lax.dot_general(member_grad, w_out, (((0,), (1,)), ((), ())), preferred_element_type=jnp.float32)
        grad_pre = (back * silu_slope(pre)).astype(jnp.bfloat16)
        grad_in = lax.dot_general(member_latent, grad_pre, (((0,), (0,)), ((), ())), preferred_element_type=jnp.float32)
        grad_out = lax.dot_general(hidden, member_grad, (((0,), (1,)), ((), ())), preferred_element_type=jnp.float32)
        return ((carry[0] + grad_in, carry[1] + grad_out), None)
    start = (jnp.zeros(w_in.shape, jnp.float32), jnp.zeros(w_out.shape, jnp.float32))
    totals, unused = lax.scan(accumulate, start, (latent, grad_fields))
    return (totals[0], totals[1])
```

```python
import functools

import jax
import jax.numpy as jnp
from jax import lax
from jax.experimental import pallas as pl
from jax.experimental.pallas import tpu as pltpu
from jax.sharding import Mesh, PartitionSpec as P

BF = jnp.bfloat16
F32 = jnp.float32
AXES = ("x", "zh", "y", "zl", "c")
LIMIT = 56 * 1024 * 1024


def params():
    return pltpu.CompilerParams(vmem_limit_bytes=LIMIT)


def mxu(a, b, da, db):
    return lax.dot_general(a, b, (((da,), (db,)), ((), ())), preferred_element_type=F32)


def decode_kernel(groups, latent_ref, w_in_ref, w_out_ref, hidden_ref, slope_ref, fields_ref):
    pre = jnp.dot(latent_ref[0], w_in_ref[...], preferred_element_type=F32)
    gate = 1.0 / (1.0 + jnp.exp(-pre))
    value = pre * gate
    hidden = value.astype(BF)
    hidden_ref[...] = hidden
    slope_ref[...] = (gate + value * (1.0 - gate)).astype(BF)
    fields = mxu(w_out_ref[...], hidden, 1, 1)
    rows = fields.shape[0] // groups
    for g in range(groups):
        fields_ref[g] = fields[g * rows : (g + 1) * rows].astype(BF)


def pair_kernel(scale, fields_ref, target_ref, mask_ref, out_ref, target_rows, value, total):
    members, rows, lanes = fields_ref.shape
    column = pl.multiple_of(lax.axis_index("x") * lanes, 128)
    row = pl.multiple_of(lax.axis_index("zh") * rows, 8)
    target_rows[...] = target_ref[:, pl.ds(column, lanes)].astype(F32)
    target = target_rows[pl.ds(row, rows), :]
    weight = mask_ref[:, pl.ds(column, lanes)].astype(F32) * scale / members
    for m in range(members):
        value[m] = fields_ref[m].astype(F32)
    total[...] = jnp.zeros_like(total)
    for r in range(0, rows, 8):
        for l in range(0, lanes, 128):
            at = (slice(r, r + 8), slice(l, l + 128))
            own = [value[(m,) + at] for m in range(members)]
            sums = [None] * members
            for i in range(members):
                for j in range(i):
                    d = own[i] - own[j]
                    k = d * lax.rsqrt(1.0 + d * d)
                    sums[i] = k if sums[i] is None else sums[i] + k
                    sums[j] = -k if sums[j] is None else sums[j] - k
            for m in range(members):
                total[(m,) + at] = sums[m]
    for m in range(members):
        d = value[m] - target
        k = d * lax.rsqrt(1.0 + d * d)
        out_ref[m] = (weight * (k - total[m] / members)).astype(BF)


def grads_kernel(latent_ref, hidden_ref, slope_ref, fields_ref, w_out_ref, keep_ref, send_ref, acc_in, acc_out):
    step = pl.program_id(0)
    groups, rows, lanes = fields_ref.shape
    grad = fields_ref[...].astype(F32).reshape(groups * rows, lanes).astype(BF)
    back = mxu(grad, w_out_ref[...], 0, 0)
    grad_pre = (back * slope_ref[...].astype(F32)).astype(BF)
    part_in = mxu(latent_ref[0], grad_pre, 0, 0)
    part_out = mxu(hidden_ref[...], grad, 0, 1)
    width = part_out.shape[1]

    @pl.when(step == 0)
    def _():
        acc_in[...] = part_in
        acc_out[...] = jnp.zeros_like(acc_out)
        acc_out[:, :width] = part_out

    @pl.when(step > 0)
    def _():
        acc_in[...] += part_in
        acc_out[:, :width] += part_out

    @pl.when(step == pl.num_programs(0) - 1)
    def _():
        first = lax.axis_index("c") == 0

        def emit(acc, low, high):
            for x in range(4):
                for y in range(4):
                    tiles = []
                    for zh in range(4):
                        at = ((x * 4 + zh) * 4 + y) * 16
                        even, odd = acc[at : at + 8, :], acc[at + 8 : at + 16, :]
                        upper = lax.broadcasted_iota(jnp.int32, even.shape, 0) < 4
                        zero = jnp.where(upper, even, pltpu.roll(odd, 4, 0))
                        one = jnp.where(upper, pltpu.roll(even, 4, 0), odd)
                        tiles.append((zero, one))
                    zero = jnp.concatenate([t[0] for t in tiles], axis=0)
                    one = jnp.concatenate([t[1] for t in tiles], axis=0)
                    keep_ref[x * 4 + y, :, low:high] = jnp.where(first, zero, one).astype(BF)
                    send_ref[x * 4 + y, :, low:high] = jnp.where(first, one, zero).astype(BF)

        emit(acc_in, 0, 1024)
        emit(acc_out, 1024, 1152)


def add_kernel(a_ref, b_ref, out_ref):
    out_ref[...] = (a_ref[...].astype(F32) + b_ref[...].astype(F32)).astype(BF)


def plane_kernel(in_ref, out_ref):
    total = in_ref[0].astype(F32)
    for p in range(1, in_ref.shape[0]):
        total += in_ref[p].astype(F32)
    for z in range(out_ref.shape[0]):
        out_ref[z] = total[4 * z : 4 * z + 4]


def last_kernel(in_ref, grad_in_ref, grad_out_ref):
    total = in_ref[0]
    for z in range(1, in_ref.shape[0]):
        total += in_ref[z]
    width = grad_in_ref.shape[1]
    grad_in_ref[...] = total[:, :width]
    grad_out_ref[...] = total[:, width : width + grad_out_ref.shape[1]]


def per_device(latent, w_in, w_out, target, cell_mask):
    _, cells, depth = latent.shape
    hidden_size, fields_n = w_out.shape
    groups = 4
    block, rows = cells // groups, fields_n // groups
    members = groups * groups
    w_out_t = w_out.T
    total_cells = cells * 16
    scale = 1.0 / float(total_cells) ** 0.5
    whole = lambda *shape: pl.BlockSpec(shape, lambda i: (0,) * len(shape))

    hidden, slope, fields = pl.pallas_call(
        functools.partial(decode_kernel, groups),
        grid=(groups,),
        in_specs=[
            pl.BlockSpec((1, block, depth), lambda i: (0, i, 0)),
            whole(depth, hidden_size),
            whole(fields_n, hidden_size),
        ],
        out_specs=[
            pl.BlockSpec((block, hidden_size), lambda i: (i, 0)),
            pl.BlockSpec((block, hidden_size), lambda i: (i, 0)),
            pl.BlockSpec((groups, rows, block), lambda i: (i, 0, 0)),
        ],
        out_shape=[
            jax.ShapeDtypeStruct((cells, hidden_size), BF),
            jax.ShapeDtypeStruct((cells, hidden_size), BF),
            jax.ShapeDtypeStruct((members, rows, block), BF),
        ],
        compiler_params=params(),
        name="decode",
    )(latent, w_in, w_out_t)

    arrived = lax.all_to_all(fields, ("x", "zh"), 0, 0, tiled=True)

    grads = pl.pallas_call(
        functools.partial(pair_kernel, scale),
        out_shape=jax.ShapeDtypeStruct((members, rows, block), BF),
        scratch_shapes=[
            pltpu.VMEM((fields_n, block), F32),
            pltpu.VMEM((members, rows, block), F32),
            pltpu.VMEM((members, rows, block), F32),
        ],
        compiler_params=params(),
        name="pair",
    )(arrived, target, cell_mask[None])

    grads = lax.all_to_all(grads, ("x", "zh"), 0, 0, tiled=True)

    wide = hidden_size + 128
    half = jax.ShapeDtypeStruct((16, 32, wide), BF)
    keep, send = pl.pallas_call(
        grads_kernel,
        grid=(groups,),
        in_specs=[
            pl.BlockSpec((1, block, depth), lambda i: (0, i, 0)),
            pl.BlockSpec((block, hidden_size), lambda i: (i, 0)),
            pl.BlockSpec((block, hidden_size), lambda i: (i, 0)),
            pl.BlockSpec((groups, rows, block), lambda i: (i, 0, 0)),
            whole(fields_n, hidden_size),
        ],
        out_specs=[whole(16, 32, wide), whole(16, 32, wide)],
        out_shape=[half, half],
        scratch_shapes=[pltpu.VMEM((depth, hidden_size), F32), pltpu.VMEM((depth, 128), F32)],
        compiler_params=params(),
        name="grads",
    )(latent, hidden, slope, grads, w_out_t)

    came = lax.ppermute(send, "c", [(0, 1), (1, 0)])
    both = pl.pallas_call(add_kernel, out_shape=half, compiler_params=params(), name="core_sum")(keep, came)
    plane = lax.all_to_all(both, ("x", "y"), 0, 0, tiled=True)
    line = pl.pallas_call(
        plane_kernel, out_shape=jax.ShapeDtypeStruct((8, 4, wide), F32), compiler_params=params(), name="plane_sum"
    )(plane)
    line = lax.all_to_all(line, ("zh", "zl"), 0, 0, tiled=True)
    return pl.pallas_call(
        last_kernel,
        out_shape=[jax.ShapeDtypeStruct((4, hidden_size), F32), jax.ShapeDtypeStruct((4, fields_n), F32)],
        compiler_params=params(),
        name="line_sum",
    )(line)


def solution(mesh):
    small = Mesh(mesh.devices.reshape(4, 4, 4, 2, 2), AXES)
    member, cell = ("x", "zh"), ("y", "zl", "c")
    in_specs = (P(member, cell, None), P(), P(), P(None, cell), P(cell))
    out_specs = (P(AXES, None), P(AXES, None))
    return jax.shard_map(per_device, mesh=small, in_specs=in_specs, out_specs=out_specs, check_vma=False)
```

```python
import functools

import jax
import jax.numpy as jnp
from jax import lax
from jax.experimental import pallas as pl
from jax.experimental.pallas import tpu as pltpu
from jax.sharding import Mesh, PartitionSpec as P

BF = jnp.bfloat16
F32 = jnp.float32
AXES = ("x", "zh", "y", "zl", "c")


def params(mib):
    return pltpu.CompilerParams(vmem_limit_bytes=mib * 1024 * 1024)


def mxu(a, b, da, db):
    return lax.dot_general(a, b, (((da,), (db,)), ((), ())), preferred_element_type=F32)


def decode_kernel(
    groups, scale, latent_ref, w_in_ref, w_out_ref, target_ref, mask_ref,
    kept_ref, other_ref, fields_ref, picked_ref, target_rows,
):
    _, rows, lanes = fields_ref.shape
    members = groups * groups

    @pl.when(pl.program_id(0) == 0)
    def _():
        column = pl.multiple_of(lax.axis_index("x") * lanes, 128)
        row = pl.multiple_of(lax.axis_index("zh") * rows, 8)
        target_rows[...] = target_ref[:, pl.ds(column, lanes)].astype(F32)
        picked_ref[:rows] = target_rows[pl.ds(row, rows), :]
        weight = mask_ref[pl.ds(column, lanes)].reshape(1, lanes).astype(F32) * scale / members
        picked_ref[rows:] = jnp.broadcast_to(weight, (8, lanes))

    pre = jnp.dot(latent_ref[0], w_in_ref[...], preferred_element_type=F32)
    gate = 1.0 / (1.0 + jnp.exp(-pre))
    value = pre * gate
    hidden = value.astype(BF)
    kept_ref[:, : hidden.shape[1]] = hidden
    slope = gate + value * (1.0 - gate)
    half = slope.shape[1] // 2
    first = lax.axis_index("c") == 0
    kept_ref[:, hidden.shape[1] :] = jnp.where(first, slope[:, :half], slope[:, half:]).astype(BF)
    other_ref[...] = jnp.where(first, slope[:, half:], slope[:, :half]).astype(BF)
    fields = mxu(w_out_ref[...], hidden, 1, 1)
    for b in range(fields.shape[1] // lanes):
        for g in range(groups):
            fields_ref[b * groups + g] = fields[g * rows : (g + 1) * rows, b * lanes : (b + 1) * lanes].astype(BF)


def pair_kernel(fields_ref, picked_ref, out_ref, value, total):
    members, rows, lanes = fields_ref.shape
    target, weight = picked_ref[:rows], picked_ref[rows : rows + 1]
    for m in range(members):
        value[m] = fields_ref[m].astype(F32)
    for r in range(0, rows, 8):
        for l in range(0, lanes, 128):
            at = (slice(r, r + 8), slice(l, l + 128))
            own = [value[(m,) + at] for m in range(members)]
            sums = [None] * members
            for i in range(members):
                for j in range(i):
                    d = own[i] - own[j]
                    k = d * lax.rsqrt(1.0 + d * d)
                    sums[i] = k if sums[i] is None else sums[i] + k
                    sums[j] = -k if sums[j] is None else sums[j] - k
            for m in range(members):
                total[(m,) + at] = sums[m]
    for m in range(members):
        d = value[m] - target
        k = d * lax.rsqrt(1.0 + d * d)
        out_ref[m] = (weight * (k - total[m] / members)).astype(BF)


def gathered(fields_ref, block, groups):
    _, rows, lanes = fields_ref.shape
    chunks = fields_ref[block * groups : (block + 1) * groups]
    return chunks.astype(F32).reshape(groups * rows, lanes).astype(BF)


def grads_kernel(
    groups, kept_hbm, other_slope_hbm, own_latent_hbm, other_latent_hbm, own_fields_ref, other_fields_ref,
    w_out_ref, sent_hbm, kept, other_slope, own_latent, other_latent, own_pre, other_pre, out_term, sent,
    sems, latent_sems, sent_sems,
):
    lanes, half = own_fields_ref.shape[2], other_slope.shape[1]
    cuts = [slice(b * lanes, (b + 1) * lanes) for b in range(groups)]

    def copies_of(which, source, into):
        return [pltpu.make_async_copy(source.at[cut], into.at[cut], sems.at[which, b]) for b, cut in enumerate(cuts)]

    kepts = copies_of(0, kept_hbm, kept)
    other_slopes = copies_of(1, other_slope_hbm, other_slope)
    latents = [
        pltpu.make_async_copy(own_latent_hbm.at[0], own_latent, latent_sems.at[0]),
        pltpu.make_async_copy(other_latent_hbm.at[0], other_latent, latent_sems.at[1]),
    ]
    for copy in kepts + other_slopes + latents:
        copy.start()

    at = pl.multiple_of(lax.axis_index("c") * half, 128)
    w_out = w_out_ref[:, pl.ds(at, half)]
    fields_n = w_out.shape[0]
    out_term[...] = jnp.zeros_like(out_term)
    for b, cut in enumerate(cuts):
        grad = gathered(own_fields_ref, b, groups)
        back = mxu(grad, w_out, 0, 0)
        kepts[b].wait()
        hidden, slope = kept[cut, : kept.shape[1] - half], kept[cut, kept.shape[1] - half :]
        own_pre[cut] = (back * slope.astype(F32)).astype(BF)
        out_term[:fields_n] += jnp.dot(grad, hidden, preferred_element_type=F32)
    for b, cut in enumerate(cuts):
        back = mxu(gathered(other_fields_ref, b, groups), w_out, 0, 0)
        other_slopes[b].wait()
        other_pre[cut] = (back * other_slope[cut].astype(F32)).astype(BF)

    for copy in latents:
        copy.wait()
    chunks, chunk_rows, _ = sent.shape
    xs = ys = groups
    quarter = own_latent.shape[1] // xs
    outs = []
    for x in range(xs):
        of_x = slice(x * quarter, (x + 1) * quarter)
        total = mxu(own_latent[:, of_x], own_pre[...], 0, 0) + mxu(other_latent[:, of_x], other_pre[...], 0, 0)
        total = total.astype(BF)
        term = out_term[:, of_x].T.astype(BF)
        for y in range(ys):
            for zh in range(chunk_rows // 16):
                rows = slice((zh * ys + y) * 16, (zh * ys + y + 1) * 16)
                into = slice(zh * 16, (zh + 1) * 16)
                sent[x * ys + y, into, :half] = total[rows]
                sent[x * ys + y, into, half:] = term[rows]
        part = pl.ds(x * ys, ys)
        outs.append(pltpu.make_async_copy(sent.at[part], sent_hbm.at[part], sent_sems.at[x]))
        outs[-1].start()
    for copy in outs:
        copy.wait()


def plane_kernel(in_ref, out_ref):
    total = in_ref[0].astype(F32)
    for p in range(1, in_ref.shape[0]):
        total += in_ref[p].astype(F32)
    rows = out_ref.shape[1]
    for z in range(out_ref.shape[0]):
        out_ref[z] = total[rows * z : rows * (z + 1)]


def last_kernel(in_ref, grad_in_ref, grad_out_ref):
    first, second = in_ref[0], in_ref[1]
    for z in range(2, in_ref.shape[0], 2):
        first += in_ref[z]
        second += in_ref[z + 1]
    half = grad_in_ref.shape[1] // 2
    grad_in_ref[:, :half] = first[:, :half]
    grad_in_ref[:, half:] = second[:, :half]
    grad_out_ref[...] = (first + second)[:, half : half + grad_out_ref.shape[1]]


def shape(*dims, dtype=BF):
    return jax.ShapeDtypeStruct(dims, dtype)


def per_device(latent, w_in, w_out, target, cell_mask):
    _, cells, depth = latent.shape
    hidden_size, fields_n = w_out.shape
    groups = 4
    block, rows = cells // groups, fields_n // groups
    members = groups * groups
    half = hidden_size // 2
    wide = half + 128
    w_out_t = w_out.T
    scale = 1.0 / float(cells * 16) ** 0.5
    whole = lambda *shape: pl.BlockSpec(shape, lambda i, *_: (0,) * len(shape))
    swap = [(0, 1), (1, 0)]
    hbm = pl.BlockSpec(memory_space=pltpu.HBM)
    vmem = pl.BlockSpec(memory_space=pltpu.VMEM)
    step = 2 * block
    halves = pl.BlockSpec((step, half), lambda i: (i, 0))

    kept, other_slope, fields, picked = pl.pallas_call(
        functools.partial(decode_kernel, groups, scale),
        grid=(cells // step,),
        in_specs=[
            pl.BlockSpec((1, step, depth), lambda i: (0, i, 0)),
            whole(depth, hidden_size),
            whole(fields_n, hidden_size),
            whole(fields_n, cells),
            whole(cells),
        ],
        out_specs=[
            pl.BlockSpec((step, hidden_size + half), lambda i: (i, 0)),
            halves,
            pl.BlockSpec((2 * groups, rows, block), lambda i: (i, 0, 0)),
            whole(rows + 8, block),
        ],
        out_shape=[
            shape(cells, hidden_size + half),
            shape(cells, half),
            shape(members, rows, block),
            shape(rows + 8, block, dtype=F32),
        ],
        scratch_shapes=[pltpu.VMEM((fields_n, block), F32)],
        compiler_params=params(58),
        name="decode",
    )(latent, w_in, w_out_t, target, cell_mask)

    arrived = lax.all_to_all(fields, ("x", "zh"), 0, 0, tiled=True)
    other_slope = lax.ppermute(other_slope, "c", swap)
    other_latent = lax.ppermute(latent, "c", swap)

    grads = pl.pallas_call(
        pair_kernel,
        out_shape=shape(members, rows, block),
        scratch_shapes=[pltpu.VMEM((members, rows, block), F32), pltpu.VMEM((members, rows, block), F32)],
        compiler_params=params(16),
        name="pair",
    )(arrived, picked)

    grads = lax.all_to_all(grads, ("x", "zh"), 0, 0, tiled=True)
    other_grads = lax.ppermute(grads, "c", swap)

    xs, ys, zs = 4, 4, 8
    chunks = (xs * ys, depth // (xs * ys), wide)
    terms = pl.pallas_call(
        functools.partial(grads_kernel, groups),
        in_specs=[hbm] * 4 + [vmem] * 3,
        out_specs=hbm,
        out_shape=shape(*chunks),
        scratch_shapes=[
            pltpu.VMEM((cells, hidden_size + half), BF),
            pltpu.VMEM((cells, half), BF),
            pltpu.VMEM((cells, depth), BF),
            pltpu.VMEM((cells, depth), BF),
            pltpu.VMEM((cells, half), BF),
            pltpu.VMEM((cells, half), BF),
            pltpu.VMEM((128, hidden_size), F32),
            pltpu.VMEM(chunks, BF),
            pltpu.SemaphoreType.DMA((2, groups)),
            pltpu.SemaphoreType.DMA((2,)),
            pltpu.SemaphoreType.DMA((xs,)),
        ],
        compiler_params=params(43),
        name="weight_grads",
    )(kept, other_slope, latent, other_latent, grads, other_grads, w_out_t)

    plane = lax.all_to_all(terms, ("x", "y"), 0, 0, tiled=True)
    line = pl.pallas_call(
        plane_kernel,
        out_shape=shape(2 * zs, 4, wide, dtype=F32),
        compiler_params=params(16),
        name="plane_sum",
    )(plane)
    line = lax.all_to_all(line, ("zh", "zl", "c"), 0, 0, tiled=True)
    return pl.pallas_call(
        last_kernel,
        out_shape=[shape(4, hidden_size, dtype=F32), shape(4, fields_n, dtype=F32)],
        compiler_params=params(16),
        name="line_sum",
    )(line)


def solution(mesh):
    small = Mesh(mesh.devices.reshape(4, 4, 4, 2, 2), AXES)
    member, cell = ("x", "zh"), ("y", "zl", "c")
    in_specs = (P(member, cell, None), P(), P(), P(None, cell), P(cell))
    out_specs = (P(AXES, None), P(AXES, None))
    return jax.shard_map(per_device, mesh=small, in_specs=in_specs, out_specs=out_specs, check_vma=False)
```

```python
import functools

import jax
import jax.numpy as jnp
from jax import lax
from jax.experimental import pallas as pl
from jax.experimental.pallas import tpu as pltpu
from jax.sharding import Mesh, PartitionSpec as P

BF = jnp.bfloat16
F32 = jnp.float32
AXES = ("x", "zh", "y", "zl", "c")


def params(mib):
    return pltpu.CompilerParams(vmem_limit_bytes=mib * 1024 * 1024)


def mxu(a, b, da, db):
    return lax.dot_general(a, b, (((da,), (db,)), ((), ())), preferred_element_type=F32)


def decode_kernel(
    groups, scale, latent_ref, w_in_ref, w_out_ref, target_ref, mask_ref,
    kept_ref, other_ref, fields_ref, picked_ref, target_rows,
):
    _, rows, lanes = fields_ref.shape
    members = groups * groups

    @pl.when(pl.program_id(0) == 0)
    def _():
        column = pl.multiple_of(lax.axis_index("x") * lanes, 128)
        row = pl.multiple_of(lax.axis_index("zh") * rows, 8)
        target_rows[...] = target_ref[:, pl.ds(column, lanes)].astype(F32)
        picked_ref[:rows] = target_rows[pl.ds(row, rows), :]
        weight = mask_ref[pl.ds(column, lanes)].reshape(1, lanes).astype(F32) * scale / members
        picked_ref[rows:] = jnp.broadcast_to(weight, (8, lanes))

    pre = jnp.dot(latent_ref[0], w_in_ref[...], preferred_element_type=F32)
    gate = 1.0 / (1.0 + jnp.exp(-pre))
    value = pre * gate
    hidden = value.astype(BF)
    kept_ref[:, : hidden.shape[1]] = hidden
    slope = gate + value * (1.0 - gate)
    half = slope.shape[1] // 2
    first = lax.axis_index("c") == 0
    kept_ref[:, hidden.shape[1] :] = jnp.where(first, slope[:, :half], slope[:, half:]).astype(BF)
    other_ref[...] = jnp.where(first, slope[:, half:], slope[:, :half]).astype(BF)
    fields = mxu(w_out_ref[...], hidden, 1, 1)
    for b in range(fields.shape[1] // lanes):
        for g in range(groups):
            fields_ref[b * groups + g] = fields[g * rows : (g + 1) * rows, b * lanes : (b + 1) * lanes].astype(BF)


def pair_kernel(fields_ref, picked_ref, out_ref, value, total):
    members, rows, lanes = fields_ref.shape
    target, weight = picked_ref[:rows], picked_ref[rows : rows + 1]
    for m in range(members):
        value[m] = fields_ref[m].astype(F32)
    for r in range(0, rows, 8):
        for l in range(0, lanes, 128):
            at = (slice(r, r + 8), slice(l, l + 128))
            own = [value[(m,) + at] for m in range(members)]
            sums = [None] * members
            for i in range(members):
                for j in range(i):
                    d = own[i] - own[j]
                    k = d * lax.rsqrt(1.0 + d * d)
                    sums[i] = k if sums[i] is None else sums[i] + k
                    sums[j] = -k if sums[j] is None else sums[j] - k
            for m in range(members):
                total[(m,) + at] = sums[m]
    for m in range(members):
        d = value[m] - target
        k = d * lax.rsqrt(1.0 + d * d)
        out_ref[m] = (weight * (k - total[m] / members)).astype(BF)


def gathered(fields_ref, block, groups):
    _, rows, lanes = fields_ref.shape
    chunks = fields_ref[block * groups : (block + 1) * groups]
    return chunks.astype(F32).reshape(groups * rows, lanes).astype(BF)


class Rows:
    def __init__(self, k, own_hbm, other_hbm, own, other, sems):
        quarter = own.shape[1]
        to = lax.rem(lax.axis_index("x") + k, 4)
        self.at = pl.ds(pl.multiple_of(to * quarter, 128), quarter)
        self.own, self.other = own, other
        self.own_copy = pltpu.make_async_copy(own_hbm.at[0, :, self.at], own, sems.at[0])
        self.other_copy = pltpu.make_async_copy(other_hbm.at[0, :, self.at], other, sems.at[1])

    def start(self):
        self.own_copy.start()
        self.other_copy.start()

    def value(self, own_pre, other_pre, out_term):
        self.own_copy.wait()
        self.other_copy.wait()
        total = mxu(self.own[...], own_pre[...], 0, 0) + mxu(self.other[...], other_pre[...], 0, 0)
        return jnp.concatenate([total, out_term[:, self.at].T], axis=1)


def grads_kernel(
    groups, kept_hbm, other_slope_hbm, own_latent_hbm, other_latent_hbm, own_fields_ref, other_fields_ref,
    w_out_ref, own_pre, other_pre, out_term, top_ref, bottom_ref, kept, other_slope, own_latent, other_latent,
    sems, latent_sems,
):
    lanes, half = own_fields_ref.shape[2], other_slope.shape[1]
    cuts = [slice(b * lanes, (b + 1) * lanes) for b in range(groups)]

    def copies_of(which, source, into):
        return [pltpu.make_async_copy(source.at[cut], into.at[cut], sems.at[which, b]) for b, cut in enumerate(cuts)]

    kepts = copies_of(0, kept_hbm, kept)
    other_slopes = copies_of(1, other_slope_hbm, other_slope)
    latents = Rows(2, own_latent_hbm, other_latent_hbm, own_latent, other_latent, latent_sems)
    for copy in kepts + other_slopes:
        copy.start()
    latents.start()

    at = pl.multiple_of(lax.axis_index("c") * half, 128)
    w_out = w_out_ref[:, pl.ds(at, half)]
    fields_n = w_out.shape[0]
    out_term[...] = jnp.zeros_like(out_term)
    for b, cut in enumerate(cuts):
        grad = gathered(own_fields_ref, b, groups)
        back = mxu(grad, w_out, 0, 0)
        kepts[b].wait()
        hidden, slope = kept[cut, : kept.shape[1] - half], kept[cut, kept.shape[1] - half :]
        own_pre[cut] = (back * slope.astype(F32)).astype(BF)
        out_term[:fields_n] += jnp.dot(grad, hidden, preferred_element_type=F32)
    for b, cut in enumerate(cuts):
        back = mxu(gathered(other_fields_ref, b, groups), w_out, 0, 0)
        other_slopes[b].wait()
        other_pre[cut] = (back * other_slope[cut].astype(F32)).astype(BF)

    total = latents.value(own_pre, other_pre, out_term)
    middle = top_ref.shape[0]
    top_ref[...] = total[:middle].astype(BF)
    bottom_ref[...] = total[middle:].astype(BF)


def rest_kernel(own_latent_hbm, other_latent_hbm, own_pre, other_pre, out_term, on_ref, back_ref, stay_ref, own_latent, other_latent, sems):
    parts = []
    for i, (k, ref) in enumerate(((1, on_ref), (3, back_ref), (0, stay_ref))):
        rows = Rows(k, own_latent_hbm, other_latent_hbm, own_latent.at[i], other_latent.at[i], sems.at[i])
        rows.start()
        parts.append((rows, ref))
    for rows, ref in parts:
        ref[...] = rows.value(own_pre, other_pre, out_term)


def pass_kernel(on_ref, back_ref, top_ref, bottom_ref, on_out, back_out):
    middle = top_ref.shape[0]
    on_out[:middle] = (on_ref[:middle] + top_ref[...].astype(F32)).astype(BF)
    on_out[middle:] = on_ref[middle:].astype(BF)
    back_out[:middle] = back_ref[:middle].astype(BF)
    back_out[middle:] = (back_ref[middle:] + bottom_ref[...].astype(F32)).astype(BF)


def x_kernel(stay_ref, on_ref, back_ref, out_ref):
    total = stay_ref[...] + on_ref[...].astype(F32) + back_ref[...].astype(F32)
    rows = out_ref.shape[1]
    for p in range(out_ref.shape[0]):
        out_ref[p] = total[rows * p : rows * (p + 1)].astype(BF)


def last_kernel(in_ref, grad_in_ref, grad_out_ref):
    first, second = in_ref[0].astype(F32), in_ref[1].astype(F32)
    for z in range(2, in_ref.shape[0], 2):
        first += in_ref[z].astype(F32)
        second += in_ref[z + 1].astype(F32)
    half = grad_in_ref.shape[1] // 2
    grad_in_ref[:, :half] = first[:, :half]
    grad_in_ref[:, half:] = second[:, :half]
    grad_out_ref[...] = (first + second)[:, half : half + grad_out_ref.shape[1]]


def shape(*dims, dtype=BF):
    return jax.ShapeDtypeStruct(dims, dtype)


def per_device(latent, w_in, w_out, target, cell_mask):
    _, cells, depth = latent.shape
    hidden_size, fields_n = w_out.shape
    groups = 4
    block, rows = cells // groups, fields_n // groups
    members = groups * groups
    half = hidden_size // 2
    wide = half + 128
    w_out_t = w_out.T
    scale = 1.0 / float(cells * 16) ** 0.5
    whole = lambda *shape: pl.BlockSpec(shape, lambda i, *_: (0,) * len(shape))
    swap = [(0, 1), (1, 0)]
    hbm = pl.BlockSpec(memory_space=pltpu.HBM)
    vmem = pl.BlockSpec(memory_space=pltpu.VMEM)
    step = 2 * block
    halves = pl.BlockSpec((step, half), lambda i: (i, 0))

    kept, other_slope, fields, picked = pl.pallas_call(
        functools.partial(decode_kernel, groups, scale),
        grid=(cells // step,),
        in_specs=[
            pl.BlockSpec((1, step, depth), lambda i: (0, i, 0)),
            whole(depth, hidden_size),
            whole(fields_n, hidden_size),
            whole(fields_n, cells),
            whole(cells),
        ],
        out_specs=[
            pl.BlockSpec((step, hidden_size + half), lambda i: (i, 0)),
            halves,
            pl.BlockSpec((2 * groups, rows, block), lambda i: (i, 0, 0)),
            whole(rows + 8, block),
        ],
        out_shape=[
            shape(cells, hidden_size + half),
            shape(cells, half),
            shape(members, rows, block),
            shape(rows + 8, block, dtype=F32),
        ],
        scratch_shapes=[pltpu.VMEM((fields_n, block), F32)],
        compiler_params=params(58),
        name="decode",
    )(latent, w_in, w_out_t, target, cell_mask)

    arrived = lax.all_to_all(fields, ("x", "zh"), 0, 0, tiled=True)
    other_slope = lax.ppermute(other_slope, "c", swap)
    other_latent = lax.ppermute(latent, "c", swap)

    grads = pl.pallas_call(
        pair_kernel,
        out_shape=shape(members, rows, block),
        scratch_shapes=[pltpu.VMEM((members, rows, block), F32), pltpu.VMEM((members, rows, block), F32)],
        compiler_params=params(16),
        name="pair",
    )(arrived, picked)

    grads = lax.all_to_all(grads, ("x", "zh"), 0, 0, tiled=True)
    other_grads = lax.ppermute(grads, "c", swap)

    quarter = depth // 4
    own_pre, other_pre, out_term, top, bottom = pl.pallas_call(
        functools.partial(grads_kernel, groups),
        in_specs=[hbm] * 4 + [vmem] * 3,
        out_shape=[
            shape(cells, half),
            shape(cells, half),
            shape(128, hidden_size, dtype=F32),
            shape(quarter // 2, wide),
            shape(quarter // 2, wide),
        ],
        scratch_shapes=[
            pltpu.VMEM((cells, hidden_size + half), BF),
            pltpu.VMEM((cells, half), BF),
            pltpu.VMEM((cells, quarter), BF),
            pltpu.VMEM((cells, quarter), BF),
            pltpu.SemaphoreType.DMA((2, groups)),
            pltpu.SemaphoreType.DMA((2,)),
        ],
        compiler_params=params(40),
        name="grad_pre",
    )(kept, other_slope, latent, other_latent, grads, other_grads, w_out_t)

    right = [(i, (i + 1) % 4) for i in range(4)]
    left = [(i, (i + 3) % 4) for i in range(4)]
    top, bottom = lax.ppermute(top, "x", right), lax.ppermute(bottom, "x", left)
    on, back, stay = pl.pallas_call(
        rest_kernel,
        in_specs=[hbm] * 2 + [vmem] * 3,
        out_shape=[shape(quarter, wide, dtype=F32)] * 3,
        scratch_shapes=[
            pltpu.VMEM((3, cells, quarter), BF),
            pltpu.VMEM((3, cells, quarter), BF),
            pltpu.SemaphoreType.DMA((3, 2)),
        ],
        compiler_params=params(24),
        cost_estimate=pl.CostEstimate(flops=12 * quarter * cells * half, bytes_accessed=12 << 20, transcendentals=0),
        name="weight_grads",
    )(latent, other_latent, own_pre, other_pre, out_term)
    on, back = pl.pallas_call(
        pass_kernel, out_shape=[shape(quarter, wide)] * 2, compiler_params=params(16), name="pass_on"
    )(on, back, top, bottom)
    on, back = lax.ppermute(on, "x", right), lax.ppermute(back, "x", left)
    line = pl.pallas_call(
        x_kernel, out_shape=shape(64, 4, wide), compiler_params=params(16), name="x_sum"
    )(stay, on, back)
    line = lax.all_to_all(line, ("zh", "y", "zl", "c"), 0, 0, tiled=True)
    return pl.pallas_call(
        last_kernel,
        out_shape=[shape(4, hidden_size, dtype=F32), shape(4, fields_n, dtype=F32)],
        compiler_params=params(16),
        name="line_sum",
    )(line)


def solution(mesh):
    small = Mesh(mesh.devices.reshape(4, 4, 4, 2, 2), AXES)
    member, cell = ("x", "zh"), ("y", "zl", "c")
    in_specs = (P(member, cell, None), P(), P(), P(None, cell), P(cell))
    out_specs = (P(AXES, None), P(AXES, None))
    return jax.shard_map(per_device, mesh=small, in_specs=in_specs, out_specs=out_specs, check_vma=False)
```

```python
import functools

import jax
import jax.numpy as jnp
from jax import lax
from jax.experimental import pallas as pl
from jax.experimental.pallas import tpu as pltpu
from jax.sharding import Mesh, PartitionSpec as P

BF = jnp.bfloat16
F32 = jnp.float32
AXES = ("x", "zh", "y", "zl", "c")


def params(mib):
    return pltpu.CompilerParams(vmem_limit_bytes=mib * 1024 * 1024)


def mxu(a, b, da, db):
    return lax.dot_general(a, b, (((da,), (db,)), ((), ())), preferred_element_type=F32)


def decode_kernel(
    groups, latent_ref, w_in_ref, w_out_ref, kept_ref, other_ref, fields_ref,
):
    _, rows, lanes = fields_ref.shape
    pre = jnp.dot(latent_ref[0], w_in_ref[...], preferred_element_type=F32)
    gate = 1.0 / (1.0 + jnp.exp(-pre))
    value = pre * gate
    hidden = value.astype(BF)
    kept_ref[:, : hidden.shape[1]] = hidden
    slope = gate + value * (1.0 - gate)
    half = slope.shape[1] // 2
    first = lax.axis_index("c") == 0
    kept_ref[:, hidden.shape[1] :] = jnp.where(first, slope[:, :half], slope[:, half:]).astype(BF)
    other_ref[...] = jnp.where(first, slope[:, half:], slope[:, :half]).astype(BF)
    fields = mxu(w_out_ref[...], hidden, 1, 1)
    for b in range(fields.shape[1] // lanes):
        for g in range(groups):
            fields_ref[b * groups + g] = fields[g * rows : (g + 1) * rows, b * lanes : (b + 1) * lanes].astype(BF)


def pair_kernel(scale, fields_ref, target_ref, mask_ref, out_ref, target_rows, value, total):
    members, rows, lanes = fields_ref.shape
    column = pl.multiple_of(lax.axis_index("x") * lanes, 128)
    row = pl.multiple_of(lax.axis_index("zh") * rows, 8)
    target_rows[...] = target_ref[:, pl.ds(column, lanes)].astype(F32)
    target = target_rows[pl.ds(row, rows), :]
    weight = mask_ref[pl.ds(column, lanes)].reshape(1, lanes).astype(F32) * scale / members
    for m in range(members):
        value[m] = fields_ref[m].astype(F32)
    for r in range(0, rows, 8):
        for l in range(0, lanes, 128):
            at = (slice(r, r + 8), slice(l, l + 128))
            own = [value[(m,) + at] for m in range(members)]
            sums = [None] * members
            for i in range(members):
                for j in range(i):
                    d = own[i] - own[j]
                    k = d * lax.rsqrt(1.0 + d * d)
                    sums[i] = k if sums[i] is None else sums[i] + k
                    sums[j] = -k if sums[j] is None else sums[j] - k
            for m in range(members):
                total[(m,) + at] = sums[m]
    for m in range(members):
        d = value[m] - target
        k = d * lax.rsqrt(1.0 + d * d)
        out_ref[m] = (weight * (k - total[m] / members)).astype(BF)


def gathered(fields_ref, block, groups):
    _, rows, lanes = fields_ref.shape
    chunks = fields_ref[block * groups : (block + 1) * groups]
    return chunks.astype(F32).reshape(groups * rows, lanes).astype(BF)


class Rows:
    def __init__(self, k, own_hbm, other_hbm, own, other, sems):
        quarter = own.shape[1]
        to = lax.rem(lax.axis_index("x") + k, 4)
        self.at = pl.ds(pl.multiple_of(to * quarter, 128), quarter)
        self.own, self.other = own, other
        self.own_copy = pltpu.make_async_copy(own_hbm.at[0, :, self.at], own, sems.at[0])
        self.other_copy = pltpu.make_async_copy(other_hbm.at[0, :, self.at], other, sems.at[1])

    def start(self):
        self.own_copy.start()
        self.other_copy.start()

    def value(self, own_pre, other_pre, out_term):
        self.own_copy.wait()
        self.other_copy.wait()
        total = mxu(self.own[...], own_pre[...], 0, 0) + mxu(self.other[...], other_pre[...], 0, 0)
        return jnp.concatenate([total, out_term[:, self.at].T], axis=1)


def own_kernel(groups, kept_hbm, fields_ref, w_out_ref, own_pre, out_term, kept, sems):
    lanes, half = fields_ref.shape[2], own_pre.shape[1]
    cuts = [slice(b * lanes, (b + 1) * lanes) for b in range(groups)]
    copies = [pltpu.make_async_copy(kept_hbm.at[cut], kept.at[cut], sems.at[b]) for b, cut in enumerate(cuts)]
    for copy in copies:
        copy.start()
    at = pl.multiple_of(lax.axis_index("c") * half, 128)
    w_out = w_out_ref[:, pl.ds(at, half)]
    fields_n = w_out.shape[0]
    out_term[...] = jnp.zeros_like(out_term)
    for b, cut in enumerate(cuts):
        grad = gathered(fields_ref, b, groups)
        back = mxu(grad, w_out, 0, 0)
        copies[b].wait()
        hidden, slope = kept[cut, : kept.shape[1] - half], kept[cut, kept.shape[1] - half :]
        own_pre[cut] = (back * slope.astype(F32)).astype(BF)
        out_term[:fields_n] += jnp.dot(grad, hidden, preferred_element_type=F32)


def other_kernel(
    groups, slope_hbm, own_latent_hbm, other_latent_hbm, fields_ref, w_out_ref, own_pre, out_term, other_pre, top_ref,
    bottom_ref, slope, own_latent, other_latent, sems, latent_sems,
):
    lanes, half = fields_ref.shape[2], own_pre.shape[1]
    cuts = [slice(b * lanes, (b + 1) * lanes) for b in range(groups)]
    copies = [pltpu.make_async_copy(slope_hbm.at[cut], slope.at[cut], sems.at[b]) for b, cut in enumerate(cuts)]
    latents = Rows(2, own_latent_hbm, other_latent_hbm, own_latent, other_latent, latent_sems)
    for copy in copies:
        copy.start()
    latents.start()
    at = pl.multiple_of(lax.axis_index("c") * half, 128)
    w_out = w_out_ref[:, pl.ds(at, half)]
    for b, cut in enumerate(cuts):
        back = mxu(gathered(fields_ref, b, groups), w_out, 0, 0)
        copies[b].wait()
        other_pre[cut] = (back * slope[cut].astype(F32)).astype(BF)
    total = latents.value(own_pre, other_pre, out_term)
    middle = top_ref.shape[0]
    top_ref[...] = total[:middle].astype(BF)
    bottom_ref[...] = total[middle:].astype(BF)


def rest_kernel(own_latent_hbm, other_latent_hbm, own_pre, other_pre, out_term, on_ref, back_ref, stay_ref, own_latent, other_latent, sems):
    parts = []
    for i, (k, ref) in enumerate(((1, on_ref), (3, back_ref), (0, stay_ref))):
        rows = Rows(k, own_latent_hbm, other_latent_hbm, own_latent.at[i], other_latent.at[i], sems.at[i])
        rows.start()
        parts.append((rows, ref))
    for rows, ref in parts:
        ref[...] = rows.value(own_pre, other_pre, out_term)


def pass_kernel(on_ref, back_ref, top_ref, bottom_ref, on_out, back_out):
    middle = top_ref.shape[0]
    on_out[:middle] = (on_ref[:middle] + top_ref[...].astype(F32)).astype(BF)
    on_out[middle:] = on_ref[middle:].astype(BF)
    back_out[:middle] = back_ref[:middle].astype(BF)
    back_out[middle:] = (back_ref[middle:] + bottom_ref[...].astype(F32)).astype(BF)


def x_kernel(stay_ref, on_ref, back_ref, out_ref):
    total = stay_ref[...] + on_ref[...].astype(F32) + back_ref[...].astype(F32)
    rows = out_ref.shape[1]
    for p in range(out_ref.shape[0]):
        out_ref[p] = total[rows * p : rows * (p + 1)].astype(BF)


def split_kernel(in_ref, keep_ref, send_ref):
    total = in_ref[0].astype(F32)
    for p in range(1, in_ref.shape[0]):
        total += in_ref[p].astype(F32)
    first = lax.axis_index("c") == 0
    keep_ref[...] = jnp.where(first, total[:4], total[4:])
    send_ref[...] = jnp.where(first, total[4:], total[:4])


def join_kernel(keep_ref, came_ref, grad_in_ref, grad_out_ref):
    keep, came = keep_ref[...], came_ref[...]
    half = grad_in_ref.shape[1] // 2
    first = lax.axis_index("c") == 0
    grad_in_ref[:, :half] = jnp.where(first, keep[:, :half], came[:, :half])
    grad_in_ref[:, half:] = jnp.where(first, came[:, :half], keep[:, :half])
    grad_out_ref[...] = (keep + came)[:, half : half + grad_out_ref.shape[1]]


def shape(*dims, dtype=BF):
    return jax.ShapeDtypeStruct(dims, dtype)


def per_device(latent, w_in, w_out, target, cell_mask):
    _, cells, depth = latent.shape
    hidden_size, fields_n = w_out.shape
    groups = 4
    block, rows = cells // groups, fields_n // groups
    members = groups * groups
    half = hidden_size // 2
    wide = half + 128
    w_out_t = w_out.T
    scale = 1.0 / float(cells * 16) ** 0.5
    whole = lambda *shape: pl.BlockSpec(shape, lambda i, *_: (0,) * len(shape))
    swap = [(0, 1), (1, 0)]
    hbm = pl.BlockSpec(memory_space=pltpu.HBM)
    vmem = pl.BlockSpec(memory_space=pltpu.VMEM)
    step = 2 * block
    halves = pl.BlockSpec((step, half), lambda i: (i, 0))

    kept, other_slope, fields = pl.pallas_call(
        functools.partial(decode_kernel, groups),
        grid=(cells // step,),
        in_specs=[
            pl.BlockSpec((1, step, depth), lambda i: (0, i, 0)),
            whole(depth, hidden_size),
            whole(fields_n, hidden_size),
        ],
        out_specs=[
            pl.BlockSpec((step, hidden_size + half), lambda i: (i, 0)),
            halves,
            pl.BlockSpec((2 * groups, rows, block), lambda i: (i, 0, 0)),
        ],
        out_shape=[
            shape(cells, hidden_size + half),
            shape(cells, half),
            shape(members, rows, block),
        ],
        compiler_params=params(58),
        name="decode",
    )(latent, w_in, w_out_t)

    latent, fields = lax.optimization_barrier((latent, fields))
    arrived = lax.all_to_all(fields, ("x", "zh"), 0, 0, tiled=True)
    other_slope = lax.ppermute(other_slope, "c", swap)
    other_latent = lax.ppermute(latent, "c", swap)

    grads = pl.pallas_call(
        functools.partial(pair_kernel, scale),
        out_shape=shape(members, rows, block),
        scratch_shapes=[
            pltpu.VMEM((fields_n, block), F32),
            pltpu.VMEM((members, rows, block), F32),
            pltpu.VMEM((members, rows, block), F32),
        ],
        compiler_params=params(16),
        name="pair",
    )(arrived, target, cell_mask)

    grads = lax.all_to_all(grads, ("x", "zh"), 0, 0, tiled=True)
    other_grads = lax.ppermute(grads, "c", swap)

    quarter = depth // 4
    own_pre, out_term = pl.pallas_call(
        functools.partial(own_kernel, groups),
        in_specs=[hbm] + [vmem] * 2,
        out_shape=[shape(cells, half), shape(128, hidden_size, dtype=F32)],
        scratch_shapes=[pltpu.VMEM((cells, hidden_size + half), BF), pltpu.SemaphoreType.DMA((groups,))],
        compiler_params=params(50),
        cost_estimate=pl.CostEstimate(flops=4 * cells * half * fields_n, bytes_accessed=6 << 20, transcendentals=0),
        name="own_grad_pre",
    )(kept, grads, w_out_t)
    other_pre, top, bottom = pl.pallas_call(
        functools.partial(other_kernel, groups),
        in_specs=[hbm] * 3 + [vmem] * 4,
        out_shape=[shape(cells, half), shape(quarter // 2, wide), shape(quarter // 2, wide)],
        scratch_shapes=[
            pltpu.VMEM((cells, half), BF),
            pltpu.VMEM((cells, quarter), BF),
            pltpu.VMEM((cells, quarter), BF),
            pltpu.SemaphoreType.DMA((groups,)),
            pltpu.SemaphoreType.DMA((2,)),
        ],
        compiler_params=params(40),
        name="other_grad_pre",
    )(other_slope, latent, other_latent, other_grads, w_out_t, own_pre, out_term)

    right = [(i, (i + 1) % 4) for i in range(4)]
    left = [(i, (i + 3) % 4) for i in range(4)]
    top, bottom = lax.ppermute(top, "x", right), lax.ppermute(bottom, "x", left)
    on, back, stay = pl.pallas_call(
        rest_kernel,
        in_specs=[hbm] * 2 + [vmem] * 3,
        out_shape=[shape(quarter, wide, dtype=F32)] * 3,
        scratch_shapes=[
            pltpu.VMEM((3, cells, quarter), BF),
            pltpu.VMEM((3, cells, quarter), BF),
            pltpu.SemaphoreType.DMA((3, 2)),
        ],
        compiler_params=params(24),
        cost_estimate=pl.CostEstimate(flops=12 * quarter * cells * half, bytes_accessed=12 << 20, transcendentals=0),
        name="weight_grads",
    )(latent, other_latent, own_pre, other_pre, out_term)
    on, back = pl.pallas_call(
        pass_kernel, out_shape=[shape(quarter, wide)] * 2, compiler_params=params(16), name="pass_on"
    )(on, back, top, bottom)
    on, back = lax.ppermute(on, "x", right), lax.ppermute(back, "x", left)
    line = pl.pallas_call(
        x_kernel, out_shape=shape(32, 8, wide), compiler_params=params(16), name="x_sum"
    )(stay, on, back)
    line = lax.all_to_all(line, ("zh", "y", "zl"), 0, 0, tiled=True)
    few = shape(4, wide, dtype=F32)
    keep, send = pl.pallas_call(split_kernel, out_shape=[few, few], compiler_params=params(16), name="yz_sum")(line)
    came = lax.ppermute(send, "c", swap)
    return pl.pallas_call(
        join_kernel,
        out_shape=[shape(4, hidden_size, dtype=F32), shape(4, fields_n, dtype=F32)],
        compiler_params=params(16),
        name="join",
    )(keep, came)


def solution(mesh):
    small = Mesh(mesh.devices.reshape(4, 4, 4, 2, 2), AXES)
    member, cell = ("x", "zh"), ("y", "zl", "c")
    in_specs = (P(member, cell, None), P(), P(), P(None, cell), P(cell))
    out_specs = (P(AXES, None), P(AXES, None))
    return jax.shard_map(per_device, mesh=small, in_specs=in_specs, out_specs=out_specs, check_vma=False)
```

```python
import functools

import jax
import jax.numpy as jnp
from jax import lax
from jax.experimental import pallas as pl
from jax.experimental.pallas import tpu as pltpu
from jax.sharding import Mesh, PartitionSpec as P

BF = jnp.bfloat16
F32 = jnp.float32
AXES = ("x", "zh", "y", "zl", "c")


def params(mib):
    return pltpu.CompilerParams(vmem_limit_bytes=mib * 1024 * 1024)


def mxu(a, b, da, db):
    return lax.dot_general(a, b, (((da,), (db,)), ((), ())), preferred_element_type=F32)


def decode_kernel(
    groups, latent_ref, w_in_ref, w_out_ref, kept_ref, other_ref, fields_ref,
):
    _, rows, lanes = fields_ref.shape
    pre = jnp.dot(latent_ref[0], w_in_ref[...], preferred_element_type=F32)
    gate = 1.0 / (1.0 + jnp.exp(-pre))
    value = pre * gate
    hidden = value.astype(BF)
    kept_ref[:, : hidden.shape[1]] = hidden
    slope = gate + value * (1.0 - gate)
    half = slope.shape[1] // 2
    first = lax.axis_index("c") == 0
    kept_ref[:, hidden.shape[1] :] = jnp.where(first, slope[:, :half], slope[:, half:]).astype(BF)
    other_ref[...] = jnp.where(first, slope[:, half:], slope[:, :half]).astype(BF)
    fields = mxu(w_out_ref[...], hidden, 1, 1)
    for b in range(fields.shape[1] // lanes):
        for g in range(groups):
            fields_ref[b * groups + g] = fields[g * rows : (g + 1) * rows, b * lanes : (b + 1) * lanes].astype(BF)


def pair_kernel(scale, fields_ref, target_ref, mask_ref, out_ref, target_rows, value, total):
    members, rows, lanes = fields_ref.shape
    column = pl.multiple_of(lax.axis_index("x") * lanes, 128)
    row = pl.multiple_of(lax.axis_index("zh") * rows, 8)
    target_rows[...] = target_ref[:, pl.ds(column, lanes)].astype(F32)
    target = target_rows[pl.ds(row, rows), :]
    weight = mask_ref[pl.ds(column, lanes)].reshape(1, lanes).astype(F32) * scale / members
    for m in range(members):
        value[m] = fields_ref[m].astype(F32)
    for r in range(0, rows, 8):
        for l in range(0, lanes, 128):
            at = (slice(r, r + 8), slice(l, l + 128))
            own = [value[(m,) + at] for m in range(members)]
            sums = [None] * members
            for i in range(members):
                for j in range(i):
                    d = own[i] - own[j]
                    k = d * lax.rsqrt(1.0 + d * d)
                    sums[i] = k if sums[i] is None else sums[i] + k
                    sums[j] = -k if sums[j] is None else sums[j] - k
            for m in range(members):
                total[(m,) + at] = sums[m]
    for m in range(members):
        d = value[m] - target
        k = d * lax.rsqrt(1.0 + d * d)
        out_ref[m] = (weight * (k - total[m] / members)).astype(BF)


def gathered(fields_ref, block, groups):
    _, rows, lanes = fields_ref.shape
    chunks = fields_ref[block * groups : (block + 1) * groups]
    return chunks.astype(F32).reshape(groups * rows, lanes).astype(BF)


class Rows:
    def __init__(self, k, own_hbm, other_hbm, own, other, sems):
        quarter = own.shape[1]
        to = lax.rem(lax.axis_index("x") + k, 4)
        self.at = pl.ds(pl.multiple_of(to * quarter, 128), quarter)
        self.own, self.other = own, other
        self.own_copy = pltpu.make_async_copy(own_hbm.at[0, :, self.at], own, sems.at[0])
        self.other_copy = pltpu.make_async_copy(other_hbm.at[0, :, self.at], other, sems.at[1])

    def start(self):
        self.own_copy.start()
        self.other_copy.start()

    def value(self, own_pre, other_pre, out_term):
        self.own_copy.wait()
        self.other_copy.wait()
        total = mxu(self.own[...], own_pre[...], 0, 0) + mxu(self.other[...], other_pre[...], 0, 0)
        return jnp.concatenate([total, out_term[:, self.at].T], axis=1)


def own_kernel(groups, kept_hbm, fields_ref, w_out_ref, own_pre, out_term, kept, sems):
    lanes, half = fields_ref.shape[2], own_pre.shape[1]
    cuts = [slice(b * lanes, (b + 1) * lanes) for b in range(groups)]
    copies = [pltpu.make_async_copy(kept_hbm.at[cut], kept.at[cut], sems.at[b]) for b, cut in enumerate(cuts)]
    for copy in copies:
        copy.start()
    at = pl.multiple_of(lax.axis_index("c") * half, 128)
    w_out = w_out_ref[:, pl.ds(at, half)]
    fields_n = w_out.shape[0]
    out_term[...] = jnp.zeros_like(out_term)
    for b, cut in enumerate(cuts):
        grad = gathered(fields_ref, b, groups)
        back = mxu(grad, w_out, 0, 0)
        copies[b].wait()
        hidden, slope = kept[cut, : kept.shape[1] - half], kept[cut, kept.shape[1] - half :]
        own_pre[cut] = (back * slope.astype(F32)).astype(BF)
        out_term[:fields_n] += jnp.dot(grad, hidden, preferred_element_type=F32)


def other_kernel(
    groups, slope_hbm, own_latent_hbm, other_latent_hbm, fields_ref, w_out_ref, own_pre, out_term, other_pre, top_ref,
    bottom_ref, slope, own_latent, other_latent, sems, latent_sems,
):
    lanes, half = fields_ref.shape[2], own_pre.shape[1]
    cuts = [slice(b * lanes, (b + 1) * lanes) for b in range(groups)]
    copies = [pltpu.make_async_copy(slope_hbm.at[cut], slope.at[cut], sems.at[b]) for b, cut in enumerate(cuts)]
    latents = Rows(2, own_latent_hbm, other_latent_hbm, own_latent, other_latent, latent_sems)
    for copy in copies:
        copy.start()
    latents.start()
    at = pl.multiple_of(lax.axis_index("c") * half, 128)
    w_out = w_out_ref[:, pl.ds(at, half)]
    for b, cut in enumerate(cuts):
        back = mxu(gathered(fields_ref, b, groups), w_out, 0, 0)
        copies[b].wait()
        other_pre[cut] = (back * slope[cut].astype(F32)).astype(BF)
    total = latents.value(own_pre, other_pre, out_term)
    middle = top_ref.shape[0]
    top_ref[...] = total[:middle].astype(BF)
    bottom_ref[...] = total[middle:].astype(BF)


def rest_kernel(own_latent_hbm, other_latent_hbm, own_pre, other_pre, out_term, on_ref, back_ref, stay_ref, own_latent, other_latent, sems):
    parts = []
    for i, (k, ref) in enumerate(((1, on_ref), (3, back_ref), (0, stay_ref))):
        rows = Rows(k, own_latent_hbm, other_latent_hbm, own_latent.at[i], other_latent.at[i], sems.at[i])
        rows.start()
        parts.append((rows, ref))
    for rows, ref in parts:
        ref[...] = rows.value(own_pre, other_pre, out_term)


def pass_kernel(on_ref, back_ref, top_ref, bottom_ref, on_out, back_out):
    middle = top_ref.shape[0]
    on_out[:middle] = (on_ref[:middle] + top_ref[...].astype(F32)).astype(BF)
    on_out[middle:] = on_ref[middle:].astype(BF)
    back_out[:middle] = back_ref[:middle].astype(BF)
    back_out[middle:] = (back_ref[middle:] + bottom_ref[...].astype(F32)).astype(BF)


def x_kernel(stay_ref, on_ref, back_ref, out_ref):
    total = stay_ref[...] + on_ref[...].astype(F32) + back_ref[...].astype(F32)
    rows = out_ref.shape[1]
    for p in range(out_ref.shape[0]):
        out_ref[p] = total[rows * p : rows * (p + 1)].astype(BF)


def split_kernel(in_ref, keep_ref, send_ref):
    total = in_ref[0].astype(F32)
    for p in range(1, in_ref.shape[0]):
        total += in_ref[p].astype(F32)
    first = lax.axis_index("c") == 0
    keep_ref[...] = jnp.where(first, total[:4], total[4:])
    send_ref[...] = jnp.where(first, total[4:], total[:4])


def join_kernel(keep_ref, came_ref, grad_in_ref, grad_out_ref):
    keep, came = keep_ref[...], came_ref[...]
    half = grad_in_ref.shape[1] // 2
    first = lax.axis_index("c") == 0
    grad_in_ref[:, :half] = jnp.where(first, keep[:, :half], came[:, :half])
    grad_in_ref[:, half:] = jnp.where(first, came[:, :half], keep[:, :half])
    grad_out_ref[...] = (keep + came)[:, half : half + grad_out_ref.shape[1]]


def shape(*dims, dtype=BF):
    return jax.ShapeDtypeStruct(dims, dtype)


def per_device(latent, w_in, w_out, target, cell_mask):
    _, cells, depth = latent.shape
    hidden_size, fields_n = w_out.shape
    groups = 4
    block, rows = cells // groups, fields_n // groups
    members = groups * groups
    half = hidden_size // 2
    wide = half + 128
    w_out_t = w_out.T
    scale = 1.0 / float(cells * 16) ** 0.5
    whole = lambda *shape: pl.BlockSpec(shape, lambda i, *_: (0,) * len(shape))
    swap = [(0, 1), (1, 0)]
    hbm = pl.BlockSpec(memory_space=pltpu.HBM)
    vmem = pl.BlockSpec(memory_space=pltpu.VMEM)
    step = 2 * block
    halves = pl.BlockSpec((step, half), lambda i: (i, 0))

    kept, other_slope, fields = pl.pallas_call(
        functools.partial(decode_kernel, groups),
        grid=(cells // step,),
        in_specs=[
            pl.BlockSpec((1, step, depth), lambda i: (0, i, 0)),
            whole(depth, hidden_size),
            whole(fields_n, hidden_size),
        ],
        out_specs=[
            pl.BlockSpec((step, hidden_size + half), lambda i: (i, 0)),
            halves,
            pl.BlockSpec((2 * groups, rows, block), lambda i: (i, 0, 0)),
        ],
        out_shape=[
            shape(cells, hidden_size + half),
            shape(cells, half),
            shape(members, rows, block),
        ],
        compiler_params=params(58),
        name="decode",
    )(latent, w_in, w_out_t)

    arrived = lax.all_to_all(fields, ("x", "zh"), 0, 0, tiled=True)
    other_slope = lax.ppermute(other_slope, "c", swap)
    other_latent = lax.ppermute(latent, "c", swap)

    grads = pl.pallas_call(
        functools.partial(pair_kernel, scale),
        out_shape=shape(members, rows, block),
        scratch_shapes=[
            pltpu.VMEM((fields_n, block), F32),
            pltpu.VMEM((members, rows, block), F32),
            pltpu.VMEM((members, rows, block), F32),
        ],
        compiler_params=params(16),
        name="pair",
    )(arrived, target, cell_mask)

    grads = lax.all_to_all(grads, ("x", "zh"), 0, 0, tiled=True)
    other_grads = lax.ppermute(grads, "c", swap)

    quarter = depth // 4
    own_pre, out_term = pl.pallas_call(
        functools.partial(own_kernel, groups),
        in_specs=[hbm] + [vmem] * 2,
        out_shape=[shape(cells, half), shape(128, hidden_size, dtype=F32)],
        scratch_shapes=[pltpu.VMEM((cells, hidden_size + half), BF), pltpu.SemaphoreType.DMA((groups,))],
        compiler_params=params(50),
        cost_estimate=pl.CostEstimate(flops=4 * cells * half * fields_n, bytes_accessed=6 << 20, transcendentals=0),
        name="own_grad_pre",
    )(kept, grads, w_out_t)
    other_pre, top, bottom = pl.pallas_call(
        functools.partial(other_kernel, groups),
        in_specs=[hbm] * 3 + [vmem] * 4,
        out_shape=[shape(cells, half), shape(quarter // 2, wide), shape(quarter // 2, wide)],
        scratch_shapes=[
            pltpu.VMEM((cells, half), BF),
            pltpu.VMEM((cells, quarter), BF),
            pltpu.VMEM((cells, quarter), BF),
            pltpu.SemaphoreType.DMA((groups,)),
            pltpu.SemaphoreType.DMA((2,)),
        ],
        compiler_params=params(40),
        name="other_grad_pre",
    )(other_slope, latent, other_latent, other_grads, w_out_t, own_pre, out_term)

    right = [(i, (i + 1) % 4) for i in range(4)]
    left = [(i, (i + 3) % 4) for i in range(4)]
    top, bottom = lax.ppermute(top, "x", right), lax.ppermute(bottom, "x", left)
    on, back, stay = pl.pallas_call(
        rest_kernel,
        in_specs=[hbm] * 2 + [vmem] * 3,
        out_shape=[shape(quarter, wide, dtype=F32)] * 3,
        scratch_shapes=[
            pltpu.VMEM((3, cells, quarter), BF),
            pltpu.VMEM((3, cells, quarter), BF),
            pltpu.SemaphoreType.DMA((3, 2)),
        ],
        compiler_params=params(24),
        cost_estimate=pl.CostEstimate(flops=12 * quarter * cells * half, bytes_accessed=12 << 20, transcendentals=0),
        name="weight_grads",
    )(latent, other_latent, own_pre, other_pre, out_term)
    on, back = pl.pallas_call(
        pass_kernel, out_shape=[shape(quarter, wide)] * 2, compiler_params=params(16), name="pass_on"
    )(on, back, top, bottom)
    on, back = lax.ppermute(on, "x", right), lax.ppermute(back, "x", left)
    line = pl.pallas_call(
        x_kernel, out_shape=shape(32, 8, wide), compiler_params=params(16), name="x_sum"
    )(stay, on, back)
    line = lax.all_to_all(line, ("zh", "y", "zl"), 0, 0, tiled=True)
    few = shape(4, wide, dtype=F32)
    keep, send = pl.pallas_call(split_kernel, out_shape=[few, few], compiler_params=params(16), name="yz_sum")(line)
    came = lax.ppermute(send, "c", swap)
    return pl.pallas_call(
        join_kernel,
        out_shape=[shape(4, hidden_size, dtype=F32), shape(4, fields_n, dtype=F32)],
        compiler_params=params(16),
        name="join",
    )(keep, came)


def solution(mesh):
    small = Mesh(mesh.devices.reshape(4, 4, 4, 2, 2), AXES)
    member, cell = ("x", "zh"), ("y", "zl", "c")
    in_specs = (P(member, cell, None), P(), P(), P(None, cell), P(cell))
    out_specs = (P(AXES, None), P(AXES, None))
    return jax.shard_map(per_device, mesh=small, in_specs=in_specs, out_specs=out_specs, check_vma=False)
```
